32 devices in a mesh: group: 4 (over z), head: 2 (over core), batch: 4 (over y, x).
Axes of the slice: x: 2, y: 2, z: 4, core: 2. Of those that a mesh axis runs over, the one named last changes fastest.
Arguments:
- queries: bfloat16 [2048, 1536], P(('batch', 'group'), 'head'), parts along dimension 0, may hold values from -6 to 6
- keys: bfloat16 [2048, 1536], P(('batch', 'group'), 'head'), parts along dimension 0, may hold values from -6 to 6
- values: bfloat16 [2048, 1536], P(('batch', 'group'), 'head'), parts along dimension 0, may hold values from -6 to 6
- grad_out: bfloat16 [2048, 1536], P(('batch', 'group'), 'head'), parts along dimension 0, may hold values from -6 to 6
- lengths: int32 [32], P('batch'), parts along dimension 0, may hold values from 20 to 64, as said below
Outputs:
- grad_queries: bfloat16 [2048, 1536], P(('batch', 'group'), 'head'), parts along dimension 0
- grad_keys: bfloat16 [2048, 1536], P(('batch', 'group'), 'head'), parts along dimension 0
- grad_values: bfloat16 [2048, 1536], P(('batch', 'group'), 'head'), parts along dimension 0
The draws below stay inside these ranges and needn't reach their ends.
There are 4 independent parts, one for each index of `batch`. The reference program is written for one: setup_inputs(seed, part) draws one part's arguments, and reference() takes and returns one part's arrays. A program takes and returns all parts, laid end to end along the dimension named above; each array names one. Nothing has to cross between parts.
Inputs may be any that keep to these rules, and one draw needn't show every extreme that they name: `lengths`: in every draw some span is full, with 64 valid tokens.
All inputs are finite; a program needn't handle non-finite values.
Results may differ from the reference program's by a relative error of at most 0.022.
Values may be sent and summed in bfloat16 or wider, within the bound.
A program may use at most 64 MiB of HBM per device.

```python
import math
import jax
import jax.numpy as jnp
from jax import lax

HD = 128
SPANS = 8
TOKENS = 512
SPAN_LEN = 64
HEADS = 12


def draw_queries(key, part):
    key = jax.random.fold_in(key, 11)
    result = jnp.clip(jax.random.normal(key, (TOKENS, HEADS * HD), jnp.float32), -4.0, 4.0)
    return result.astype(jnp.bfloat16)


def draw_keys(key, part):
    key = jax.random.fold_in(key, 23)
    result = jnp.clip(jax.random.normal(key, (TOKENS, HEADS * HD), jnp.float32), -4.0, 4.0)
    return result.astype(jnp.bfloat16)


def draw_lengths(key, part):
    key = jax.random.fold_in(key, 37)
    drawn = jax.random.randint(key, (SPANS,), SPAN_LEN // 4 + 4, SPAN_LEN + 1, dtype=jnp.int32)
    full_span = jax.random.randint(jax.random.fold_in(key, 5), (), 0, SPANS, dtype=jnp.int32)
    return jnp.where(jnp.arange(SPANS, dtype=jnp.int32) == full_span, SPAN_LEN, drawn).astype(jnp.int32)


def levels(rng, dims, shards, least, largest):
    loudness, own = 1.0, jax.random.fold_in(rng, 6)
    for dim, shards_of in shards:
        steps = jnp.exp(jax.random.uniform(jax.random.fold_in(own, dim), (shards_of,), jnp.float32, least / len(shards), largest / len(shards)))
        loudness = loudness * jnp.repeat(steps, dims[dim] // shards_of).reshape([-1 if axis == dim else 1 for axis in range(len(dims))])
    return loudness


def normal_values(stream_key, extent, width, most, pieces=(), kind=jnp.bfloat16):
    array = jax.random.normal(stream_key, extent, jnp.float32) * width
    if len(pieces) > 0:
        array = levels(stream_key, extent, pieces, -0.22, 0.18) * array
    return jnp.clip(array, min=-most, max=most).astype(kind)


def setup_inputs(seed: int = 0, part: int = 0) -> dict:
    seeds = jax.random.split(jax.random.key(seed), 6)
    part_keys = jax.random.split(jax.random.fold_in(seeds[5], part), 6)
    return {
        "queries": draw_queries(jax.random.fold_in(jax.random.fold_in(seeds[5], part), 71), part),
        "keys": draw_keys(jax.random.fold_in(jax.random.fold_in(seeds[5], part), 71), part),
        "values": normal_values(part_keys[2], (TOKENS, HEADS * HD), 1.0, 6.0, ((0, 4), (1, 2))),
        "grad_out": normal_values(part_keys[3], (TOKENS, HEADS * HD), 1.0, 6.0, ((0, 4), (1, 2))),
        "lengths": draw_lengths(jax.random.fold_in(jax.random.fold_in(seeds[5], part), 71), part),
    }


masked_score = -1e+30

def reference(queries, keys, values, grad_out, lengths):
    score_scale = 1.0 / math.sqrt(HD)
    token_index = jnp.arange(TOKENS, dtype=jnp.int32)
    token_span = token_index // SPAN_LEN
    token_valid = token_index % SPAN_LEN < lengths[token_span]
    visible = (token_span[None, :] <= token_span[:, None]) & token_valid[None, :]
    grad_kept = jnp.where(token_valid[:, None], grad_out, jnp.zeros_like(grad_out))

    def split_heads(matrix):
        return matrix.reshape(TOKENS, HEADS, HD).transpose(1, 0, 2)

    def join_heads(tensor):
        return tensor.transpose(1, 0, 2).reshape(TOKENS, HEADS * HD)

    def one_head(head_parts):
        query_head, key_head, value_head, grad_head = head_parts
        scores = jnp.dot(query_head, key_head.T, preferred_element_type=jnp.float32) * score_scale
        scores = jnp.where(visible, scores, masked_score)
        row_max = lax.optimization_barrier(jnp.max(scores, axis=1, keepdims=True))
        unnormed = jnp.exp(scores - row_max)
        probs = unnormed / lax.optimization_barrier(jnp.sum(unnormed, axis=1, keepdims=True))
        probs_low = probs.astype(jnp.bfloat16)
        attended = jnp.dot(probs_low, value_head, preferred_element_type=jnp.float32).astype(jnp.bfloat16)
        row_delta = lax.optimization_barrier(jnp.sum(grad_head.astype(jnp.float32) * attended.astype(jnp.float32), axis=1, keepdims=True))
        prob_grad = jnp.dot(grad_head, value_head.T, preferred_element_type=jnp.float32)
        score_grad = (probs * (prob_grad - row_delta)).astype(jnp.bfloat16)
        query_grad = (jnp.dot(score_grad, key_head, preferred_element_type=jnp.float32) * score_scale).astype(jnp.bfloat16)
        key_grad = (jnp.dot(score_grad.T, query_head, preferred_element_type=jnp.float32) * score_scale).astype(jnp.bfloat16)
        value_grad = jnp.dot(probs_low.T, grad_head, preferred_element_type=jnp.float32).astype(jnp.bfloat16)
        return (query_grad, key_grad, value_grad)
    query_grads, key_grads, value_grads = lax.map(one_head, (split_heads(queries), split_heads(keys), split_heads(values), split_heads(grad_kept)))
    return (join_heads(query_grads), join_heads(key_grads), join_heads(value_grads))
```

```python
import functools
import math

import jax
import jax.numpy as jnp
from jax import lax
from jax.experimental import pallas as pl
from jax.experimental.pallas import tpu as pltpu
from jax.sharding import PartitionSpec as P

HD = 128


masked_score = -1e30


def passed_along(block, axis, distance):
    devices = range(lax.axis_size(axis))
    route = [((i - distance) % len(devices), i) for i in devices]
    return lax.ppermute(block, axis, route)


def lookup_length(span_ids, lengths):
    table = jnp.arange(lengths.shape[0], dtype=jnp.int32)
    return jnp.sum(jnp.where(span_ids[:, None] == table[None, :], lengths[None, :], 0), axis=1)


def heads_first(matrix, head_count):
    return matrix.reshape(matrix.shape[0], head_count, HD).transpose(1, 0, 2)


def rows_first(tensor):
    return tensor.transpose(1, 0, 2).reshape(tensor.shape[1], tensor.shape[0] * tensor.shape[2])


def body(queries, keys, values, grad_out, lengths):
    row_count, feature_count = queries.shape
    head_count = feature_count // HD
    slice_count = lax.axis_size("group")
    my_slice = lax.axis_index("group")
    score_scale = 1.0 / math.sqrt(HD)
    gathered_keys, gathered_values = (
        lax.all_gather(keys, "group", axis=0, tiled=True),
        lax.all_gather(values, "group", axis=0, tiled=True),
    )
    key_count = gathered_keys.shape[0]
    span_len = key_count // lengths.shape[0]
    key_index = jnp.arange(key_count, dtype=jnp.int32)
    key_span = key_index // span_len
    key_valid = key_index % span_len < lookup_length(key_span, lengths)
    own_index = my_slice * row_count + jnp.arange(row_count, dtype=jnp.int32)
    own_span = own_index // span_len
    own_valid = own_index % span_len < lookup_length(own_span, lengths)
    grad_kept = jnp.where(own_valid[:, None], grad_out, jnp.zeros_like(grad_out))
    top_span = jnp.max(own_span)
    query_heads = heads_first(queries, head_count)
    grad_heads = heads_first(grad_kept, head_count)
    key_heads = heads_first(gathered_keys, head_count)
    value_heads = heads_first(gathered_values, head_count)
    visible = (key_span[None, :] <= own_span[:, None]) & key_valid[None, :]

    def row_stats(head_parts):
        query_head, grad_head, key_head, value_head = head_parts
        scores = (
            jnp.einsum("rd,kd->rk", query_head, key_head, preferred_element_type=jnp.float32)
            * score_scale
        )
        scores = jnp.where(visible, scores, masked_score)
        row_max = jnp.max(scores, axis=1, keepdims=True)
        unnormed = jnp.exp(scores - row_max)
        row_sum = jnp.sum(unnormed, axis=1, keepdims=True)
        probs_low = (unnormed / row_sum).astype(jnp.bfloat16)
        attended = jnp.dot(probs_low, value_head, preferred_element_type=jnp.float32).astype(
            jnp.bfloat16
        )
        row_delta = jnp.sum(grad_head.astype(jnp.float32) * attended.astype(jnp.float32), axis=1)
        return (row_max[:, 0], row_sum[:, 0], row_delta)

    row_max, row_sum, row_delta = lax.map(
        row_stats, (query_heads, grad_heads, key_heads, value_heads)
    )

    def dense_terms(block):
        start = block * row_count
        key_block = lax.dynamic_slice_in_dim(key_heads, start, row_count, 1)
        value_block = lax.dynamic_slice_in_dim(value_heads, start, row_count, 1)
        valid_block = lax.dynamic_slice_in_dim(key_valid, start, row_count, 0)
        span_block = lax.dynamic_slice_in_dim(key_span, start, row_count, 0)
        block_mask = (span_block[None, :] <= own_span[:, None]) & valid_block[None, :]
        scores = (
            jnp.einsum("hrd,hkd->hrk", query_heads, key_block, preferred_element_type=jnp.float32)
            * score_scale
        )
        scores = jnp.where(block_mask[None], scores, masked_score)
        probs = jnp.exp(scores - row_max[:, :, None]) / row_sum[:, :, None]
        probs_low = probs.astype(jnp.bfloat16)
        prob_grad = jnp.einsum(
            "hrd,hkd->hrk", grad_heads, value_block, preferred_element_type=jnp.float32
        )
        score_grad = (probs * (prob_grad - row_delta[:, :, None])).astype(jnp.bfloat16)
        query_term = jnp.einsum(
            "hrk,hkd->hrd", score_grad, key_block, preferred_element_type=jnp.float32
        )
        key_term = rows_first(
            jnp.einsum("hrk,hrd->hkd", score_grad, query_heads, preferred_element_type=jnp.float32)
            * score_scale
        )
        value_term = rows_first(
            jnp.einsum("hrk,hrd->hkd", probs_low, grad_heads, preferred_element_type=jnp.float32)
        )
        return (query_term, key_term, value_term)

    def empty_terms(block):
        query_term = jnp.zeros((head_count, row_count, HD), jnp.float32)
        other_term = jnp.zeros((row_count, feature_count), jnp.float32)
        return (query_term, other_term, other_term)

    def block_terms(block):
        first_span = block * row_count // span_len
        return lax.cond(first_span <= top_span, dense_terms, empty_terms, block)

    query_zero = jnp.zeros((head_count, row_count, HD), jnp.float32)

    def chain_step(block_step, loop_state):
        query_grad, travel = loop_state
        block = (my_slice - block_step) % slice_count
        query_term, key_term, value_term = block_terms(block)
        travel = travel + jnp.stack([key_term, value_term])
        travel = passed_along(travel.astype(jnp.bfloat16), "group", 1).astype(travel.dtype)
        return (query_grad + query_term, travel)

    travel_zero = jnp.zeros((2, row_count, feature_count), jnp.float32)
    query_grad, travel = lax.fori_loop(0, slice_count, chain_step, (query_zero, travel_zero))
    key_grad = travel[0]
    value_grad = travel[1]
    query_low = rows_first(query_grad * score_scale).astype(jnp.bfloat16)
    return (query_low, key_grad.astype(jnp.bfloat16), value_grad.astype(jnp.bfloat16))

MESH = pl.DeviceIdType.MESH
EXP_SCALE = 1.4426950408889634 / math.sqrt(HD)
SCALE = 1.0 / math.sqrt(HD)


def dot_nt(a, b):
    return lax.dot_general(a, b, (((1,), (1,)), ((), ())), preferred_element_type=jnp.float32)


def dot_nn(a, b):
    return lax.dot_general(a, b, (((1,), (0,)), ((), ())), preferred_element_type=jnp.float32)


def dot_tn(a, b):
    return lax.dot_general(a, b, (((0,), (0,)), ((), ())), preferred_element_type=jnp.float32)


def head_grads(query, grad, key, value, bias):
    scores = dot_nt(key, query) * EXP_SCALE + bias
    top = jnp.max(scores, axis=0, keepdims=True)
    unnormed = jnp.exp2(scores - top)
    total = jnp.sum(unnormed, axis=0, keepdims=True)
    probs = unnormed * (1.0 / total)
    prob_grad = dot_nt(value, grad)
    delta = jnp.sum(probs * prob_grad, axis=0, keepdims=True)
    score_grad = (probs * (prob_grad - delta)).astype(jnp.bfloat16)
    value_grad = dot_nn(probs.astype(jnp.bfloat16), grad)
    key_grad = dot_nn(score_grad, query) * SCALE
    query_grad = dot_tn(score_grad, key) * SCALE
    return query_grad, key_grad, value_grad


def columns(head):
    return pl.ds(pl.multiple_of(head * HD, HD), HD)


def kernel(
    head_count, lengths, q_hbm, k_hbm, v_hbm, g_hbm, dq_hbm, dk_hbm, dv_hbm,
    q_own, k_own, v_own, g_own, landed, back, partial, own_sum, done, bias, kept,
    load_sem, send_sem, land_sem, partial_send, partial_recv, final_send, final_recv, store_sem,
):
    me = lax.axis_index("group")
    rows = q_hbm.shape[0]
    spans = lengths.shape[0]
    span_len = 4 * rows // spans
    inputs = ((k_hbm, k_own), (v_hbm, v_own), (q_hbm, q_own), (g_hbm, g_own))
    outputs = (dq_hbm, dk_hbm, dv_hbm)

    def load(which):
        return pltpu.make_async_copy(inputs[which][0], inputs[which][1], load_sem.at[which])

    def store(which, head):
        return pltpu.make_async_copy(
            done.at[which, head], outputs[which].at[:, columns(head)], store_sem.at[which, head]
        )

    def forward(which, slot, sender_slot, target, head):
        return pltpu.make_async_remote_copy(
            src_ref=inputs[which][0].at[:, columns(head)],
            dst_ref=landed.at[slot, head],
            send_sem=send_sem.at[sender_slot, head],
            recv_sem=land_sem.at[slot, head],
            device_id={"group": target},
            device_id_type=MESH,
        )

    def give_back(pair, lane, target, head):
        return pltpu.make_async_remote_copy(
            src_ref=back.at[pair, head],
            dst_ref=partial.at[lane, head],
            send_sem=partial_send.at[pair, head],
            recv_sem=partial_recv.at[lane, head],
            device_id={"group": target},
            device_id_type=MESH,
        )

    def finish(which, head):
        return pltpu.make_async_remote_copy(
            src_ref=done.at[3 + which, head],
            dst_ref=outputs[which].at[:, columns(head)],
            send_sem=final_send.at[which, head],
            recv_sem=final_recv.at[which, head],
            device_id={"group": 3},
            device_id_type=MESH,
        )

    def greet(peers):
        barrier = pltpu.get_barrier_semaphore()
        for peer in peers:
            pl.semaphore_signal(barrier, inc=1, device_id={"group": peer}, device_id_type=MESH)
        pl.semaphore_wait(barrier, len(peers))

    def each_head(step):
        lax.fori_loop(0, head_count, lambda head, carry: (step(head), carry)[1], 0)

    def make_masks(first_query, query_count, key_count):
        shape = (key_count, query_count)
        key_at = lax.broadcasted_iota(jnp.int32, shape, 0)
        query_at = lax.broadcasted_iota(jnp.int32, shape, 1) + first_query
        row_at = lax.broadcasted_iota(jnp.int32, (query_count, HD), 0) + first_query
        key_span = jnp.zeros(shape, jnp.int32)
        query_span = jnp.zeros(shape, jnp.int32)
        key_end = jnp.zeros(shape, jnp.int32)
        row_end = jnp.zeros((query_count, HD), jnp.int32)
        for span in range(spans):
            start = span * span_len
            end = start + lengths[span]
            key_span = jnp.where(key_at >= start, span, key_span)
            query_span = jnp.where(query_at >= start, span, query_span)
            key_end = jnp.where(key_at >= start, end, key_end)
            row_end = jnp.where(row_at >= start, end, row_end)
        visible = (key_span <= query_span) & (key_at < key_end)
        bias[:key_count, :query_count] = jnp.where(visible, 0.0, masked_score)
        kept[:query_count, :] = jnp.where(row_at < row_end, 1.0, 0.0).astype(jnp.bfloat16)

    for which in range(4):
        load(which).start()

    def wait_loads():
        for which in range(4):
            load(which).wait()

    def low(value):
        return value.astype(jnp.bfloat16)

    @pl.when(me == 0)
    def _():
        greet((1, 2))

        def send(head):
            for which in range(2):
                forward(which, which, which, 2, head).start()
            for which in range(2):
                forward(which, which, 2 + which, 1, head).start()

        each_head(send)
        make_masks(0, rows, rows)
        wait_loads()

        def own(head):
            at = columns(head)
            dq, dk, dv = head_grads(
                q_own[:, at], g_own[:, at] * kept[:rows, :], k_own[:, at], v_own[:, at],
                bias[:rows, :rows],
            )
            done[0, head] = low(dq)
            own_sum[0, head] = dk
            own_sum[1, head] = dv
            store(0, head).start()

        each_head(own)

        def gather(head):
            give_back(0, 0, 0, head).wait_recv()
            give_back(0, 1, 0, head).wait_recv()
            for which in range(2):
                done[1 + which, head] = low(
                    own_sum[which, head]
                    + partial[0, head, which].astype(jnp.float32)
                    + partial[1, head, which].astype(jnp.float32)
                )
                store(1 + which, head).start()

        each_head(gather)

        def settle(head):
            for which in range(2):
                forward(which, which, which, 2, head).wait_send()
                forward(which, which, 2 + which, 1, head).wait_send()
            for which in range(3):
                store(which, head).wait()

        each_head(settle)

    @pl.when(me == 1)
    def _():
        greet((0, 2))

        def send(head):
            for which in range(2):
                forward(which, 2 + which, which, 2, head).start()

        each_head(send)
        make_masks(rows, rows, 2 * rows)
        wait_loads()

        def work(head):
            at = columns(head)
            for which in range(2):
                forward(which, which, 2 + which, 1, head).wait_recv()
            dq, dk, dv = head_grads(
                q_own[:, at], g_own[:, at] * kept[:rows, :],
                jnp.concatenate([landed[0, head], k_own[:, at]], axis=0),
                jnp.concatenate([landed[1, head], v_own[:, at]], axis=0),
                bias[: 2 * rows, :rows],
            )
            back[0, head, 0] = low(dk[:rows])
            back[0, head, 1] = low(dv[:rows])
            give_back(0, 0, 0, head).start()
            own_sum[0, head] = dk[rows:]
            own_sum[1, head] = dv[rows:]
            done[0, head] = low(dq)
            store(0, head).start()

        each_head(work)

        def gather(head):
            give_back(1, 0, 1, head).wait_recv()
            for which in range(2):
                done[1 + which, head] = low(
                    own_sum[which, head] + partial[0, head, which].astype(jnp.float32)
                )
                store(1 + which, head).start()

        each_head(gather)

        def settle(head):
            for which in range(2):
                forward(which, 2 + which, which, 2, head).wait_send()
            give_back(0, 0, 0, head).wait_send()
            for which in range(3):
                store(which, head).wait()

        each_head(settle)

    @pl.when(me == 2)
    def _():
        greet((0, 1, 3))
        make_masks(2 * rows, 2 * rows, 4 * rows)
        wait_loads()

        def work(head):
            at = columns(head)
            for slot in range(4):
                forward(slot % 2, slot, slot, 2, head).wait_recv()
            for which in range(4):
                forward(which, 4 + which, which, 2, head).wait_recv()
            dq, dk, dv = head_grads(
                jnp.concatenate([q_own[:, at], landed[6, head]], axis=0),
                jnp.concatenate([g_own[:, at], landed[7, head]], axis=0) * kept[...],
                jnp.concatenate(
                    [landed[0, head], landed[2, head], k_own[:, at], landed[4, head]], axis=0
                ),
                jnp.concatenate(
                    [landed[1, head], landed[3, head], v_own[:, at], landed[5, head]], axis=0
                ),
                bias[...],
            )
            for target in range(2):
                mine = slice(target * rows, (target + 1) * rows)
                back[target, head, 0] = low(dk[mine])
                back[target, head, 1] = low(dv[mine])
                give_back(target, 1 - target, target, head).start()
            for which, grad in ((1, dk), (2, dv)):
                done[which, head] = low(grad[2 * rows : 3 * rows])
                done[3 + which, head] = low(grad[3 * rows :])
            done[0, head] = low(dq[:rows])
            done[3, head] = low(dq[rows:])
            for which in range(3):
                finish(which, head).start()
                store(which, head).start()

        each_head(work)

        def settle(head):
            for target in range(2):
                give_back(target, 1 - target, target, head).wait_send()
            for which in range(3):
                finish(which, head).wait_send()
                store(which, head).wait()

        each_head(settle)

    @pl.when(me == 3)
    def _():
        greet((2,))

        def send(head):
            for which in range(4):
                forward(which, 4 + which, which, 2, head).start()

        each_head(send)
        wait_loads()

        def settle(head):
            for which in range(4):
                forward(which, 4 + which, which, 2, head).wait_send()
            for which in range(3):
                finish(which, head).wait_recv()

        each_head(settle)


def four_slices(queries, keys, values, grad_out, lengths):
    rows, features = queries.shape
    heads = features // HD
    low_type = jnp.bfloat16
    out = jax.ShapeDtypeStruct((rows, features), low_type)
    anywhere = pl.BlockSpec(memory_space=pl.ANY)
    dma = pltpu.SemaphoreType.DMA
    return pl.pallas_call(
        functools.partial(kernel, heads),
        out_shape=(out, out, out),
        in_specs=[pl.BlockSpec(memory_space=pltpu.SMEM)] + [anywhere] * 4,
        out_specs=(anywhere,) * 3,
        scratch_shapes=[
            pltpu.VMEM((rows, features), low_type),
            pltpu.VMEM((rows, features), low_type),
            pltpu.VMEM((rows, features), low_type),
            pltpu.VMEM((rows, features), low_type),
            pltpu.VMEM((8, heads, rows, HD), low_type),
            pltpu.VMEM((2, heads, 2, rows, HD), low_type),
            pltpu.VMEM((2, heads, 2, rows, HD), low_type),
            pltpu.VMEM((2, heads, rows, HD), jnp.float32),
            pltpu.VMEM((6, heads, rows, HD), low_type),
            pltpu.VMEM((4 * rows, 2 * rows), jnp.float32),
            pltpu.VMEM((2 * rows, HD), low_type),
            dma((4,)),
            dma((4, heads)),
            dma((8, heads)),
            dma((2, heads)),
            dma((2, heads)),
            dma((3, heads)),
            dma((3, heads)),
            dma((3, heads)),
        ],
        compiler_params=pltpu.CompilerParams(
            collective_id=0, has_side_effects=True, vmem_limit_bytes=40 * 1024 * 1024
        ),
    )(lengths, queries, keys, values, grad_out)


def solution(mesh):
    return jax.shard_map(
        four_slices if mesh.shape["group"] == 4 else body,
        mesh=mesh,
        in_specs=(
            P(("batch", "group"), "head"),
            P(("batch", "group"), "head"),
            P(("batch", "group"), "head"),
            P(("batch", "group"), "head"),
            P("batch"),
        ),
        out_specs=(
            P(("batch", "group"), "head"),
            P(("batch", "group"), "head"),
            P(("batch", "group"), "head"),
        ),
        check_vma=False,
    )
```

```python
import functools
import math

import jax
import jax.numpy as jnp
from jax import lax
from jax.experimental import pallas as pl
from jax.experimental.pallas import tpu as pltpu
from jax.sharding import PartitionSpec as P

HD = 128


masked_score = -1e30


def passed_along(block, axis, distance):
    devices = range(lax.axis_size(axis))
    route = [((i - distance) % len(devices), i) for i in devices]
    return lax.ppermute(block, axis, route)


def lookup_length(span_ids, lengths):
    table = jnp.arange(lengths.shape[0], dtype=jnp.int32)
    return jnp.sum(jnp.where(span_ids[:, None] == table[None, :], lengths[None, :], 0), axis=1)


def heads_first(matrix, head_count):
    return matrix.reshape(matrix.shape[0], head_count, HD).transpose(1, 0, 2)


def rows_first(tensor):
    return tensor.transpose(1, 0, 2).reshape(tensor.shape[1], tensor.shape[0] * tensor.shape[2])


def body(queries, keys, values, grad_out, lengths):
    row_count, feature_count = queries.shape
    head_count = feature_count // HD
    slice_count = lax.axis_size("group")
    my_slice = lax.axis_index("group")
    score_scale = 1.0 / math.sqrt(HD)
    gathered_keys, gathered_values = (
        lax.all_gather(keys, "group", axis=0, tiled=True),
        lax.all_gather(values, "group", axis=0, tiled=True),
    )
    key_count = gathered_keys.shape[0]
    span_len = key_count // lengths.shape[0]
    key_index = jnp.arange(key_count, dtype=jnp.int32)
    key_span = key_index // span_len
    key_valid = key_index % span_len < lookup_length(key_span, lengths)
    own_index = my_slice * row_count + jnp.arange(row_count, dtype=jnp.int32)
    own_span = own_index // span_len
    own_valid = own_index % span_len < lookup_length(own_span, lengths)
    grad_kept = jnp.where(own_valid[:, None], grad_out, jnp.zeros_like(grad_out))
    top_span = jnp.max(own_span)
    query_heads = heads_first(queries, head_count)
    grad_heads = heads_first(grad_kept, head_count)
    key_heads = heads_first(gathered_keys, head_count)
    value_heads = heads_first(gathered_values, head_count)
    visible = (key_span[None, :] <= own_span[:, None]) & key_valid[None, :]

    def row_stats(head_parts):
        query_head, grad_head, key_head, value_head = head_parts
        scores = (
            jnp.einsum("rd,kd->rk", query_head, key_head, preferred_element_type=jnp.float32)
            * score_scale
        )
        scores = jnp.where(visible, scores, masked_score)
        row_max = jnp.max(scores, axis=1, keepdims=True)
        unnormed = jnp.exp(scores - row_max)
        row_sum = jnp.sum(unnormed, axis=1, keepdims=True)
        probs_low = (unnormed / row_sum).astype(jnp.bfloat16)
        attended = jnp.dot(probs_low, value_head, preferred_element_type=jnp.float32).astype(
            jnp.bfloat16
        )
        row_delta = jnp.sum(grad_head.astype(jnp.float32) * attended.astype(jnp.float32), axis=1)
        return (row_max[:, 0], row_sum[:, 0], row_delta)

    row_max, row_sum, row_delta = lax.map(
        row_stats, (query_heads, grad_heads, key_heads, value_heads)
    )

    def dense_terms(block):
        start = block * row_count
        key_block = lax.dynamic_slice_in_dim(key_heads, start, row_count, 1)
        value_block = lax.dynamic_slice_in_dim(value_heads, start, row_count, 1)
        valid_block = lax.dynamic_slice_in_dim(key_valid, start, row_count, 0)
        span_block = lax.dynamic_slice_in_dim(key_span, start, row_count, 0)
        block_mask = (span_block[None, :] <= own_span[:, None]) & valid_block[None, :]
        scores = (
            jnp.einsum("hrd,hkd->hrk", query_heads, key_block, preferred_element_type=jnp.float32)
            * score_scale
        )
        scores = jnp.where(block_mask[None], scores, masked_score)
        probs = jnp.exp(scores - row_max[:, :, None]) / row_sum[:, :, None]
        probs_low = probs.astype(jnp.bfloat16)
        prob_grad = jnp.einsum(
            "hrd,hkd->hrk", grad_heads, value_block, preferred_element_type=jnp.float32
        )
        score_grad = (probs * (prob_grad - row_delta[:, :, None])).astype(jnp.bfloat16)
        query_term = jnp.einsum(
            "hrk,hkd->hrd", score_grad, key_block, preferred_element_type=jnp.float32
        )
        key_term = rows_first(
            jnp.einsum("hrk,hrd->hkd", score_grad, query_heads, preferred_element_type=jnp.float32)
            * score_scale
        )
        value_term = rows_first(
            jnp.einsum("hrk,hrd->hkd", probs_low, grad_heads, preferred_element_type=jnp.float32)
        )
        return (query_term, key_term, value_term)

    def empty_terms(block):
        query_term = jnp.zeros((head_count, row_count, HD), jnp.float32)
        other_term = jnp.zeros((row_count, feature_count), jnp.float32)
        return (query_term, other_term, other_term)

    def block_terms(block):
        first_span = block * row_count // span_len
        return lax.cond(first_span <= top_span, dense_terms, empty_terms, block)

    query_zero = jnp.zeros((head_count, row_count, HD), jnp.float32)

    def chain_step(block_step, loop_state):
        query_grad, travel = loop_state
        block = (my_slice - block_step) % slice_count
        query_term, key_term, value_term = block_terms(block)
        travel = travel + jnp.stack([key_term, value_term])
        travel = passed_along(travel.astype(jnp.bfloat16), "group", 1).astype(travel.dtype)
        return (query_grad + query_term, travel)

    travel_zero = jnp.zeros((2, row_count, feature_count), jnp.float32)
    query_grad, travel = lax.fori_loop(0, slice_count, chain_step, (query_zero, travel_zero))
    key_grad = travel[0]
    value_grad = travel[1]
    query_low = rows_first(query_grad * score_scale).astype(jnp.bfloat16)
    return (query_low, key_grad.astype(jnp.bfloat16), value_grad.astype(jnp.bfloat16))

MESH = pl.DeviceIdType.MESH
EXP_SCALE = 1.4426950408889634 / math.sqrt(HD)
SCALE = 1.0 / math.sqrt(HD)


def dot_nt(a, b):
    return lax.dot_general(a, b, (((1,), (1,)), ((), ())), preferred_element_type=jnp.float32)


def dot_nn(a, b):
    return lax.dot_general(a, b, (((1,), (0,)), ((), ())), preferred_element_type=jnp.float32)


def dot_tn(a, b):
    return lax.dot_general(a, b, (((0,), (0,)), ((), ())), preferred_element_type=jnp.float32)


def head_grads(query, grad, key, value, bias):
    scores = dot_nt(key, query) * EXP_SCALE + bias
    top = jnp.max(scores, axis=0, keepdims=True)
    unnormed = jnp.exp2(scores - top)
    total = jnp.sum(unnormed, axis=0, keepdims=True)
    probs = unnormed * (1.0 / total)
    prob_grad = dot_nt(value, grad)
    delta = jnp.sum(probs * prob_grad, axis=0, keepdims=True)
    score_grad = (probs * (prob_grad - delta)).astype(jnp.bfloat16)
    value_grad = dot_nn(probs.astype(jnp.bfloat16), grad)
    key_grad = dot_nn(score_grad, query) * SCALE
    query_grad = dot_tn(score_grad, key) * SCALE
    return query_grad, key_grad, value_grad


def columns(head):
    return pl.ds(pl.multiple_of(head * HD, HD), HD)


def kernel(
    head_count, lengths, q_hbm, k_hbm, v_hbm, g_hbm, dq_hbm, dk_hbm, dv_hbm,
    q_own, k_own, v_own, g_own, landed, back, partial, own_sum, done, bias, kept,
    load_sem, send_sem, land_sem, partial_send, partial_recv, final_send, final_recv, store_sem,
):
    me = lax.axis_index("group")
    rows = q_hbm.shape[0]
    spans = lengths.shape[0]
    span_len = 4 * rows // spans
    inputs = ((k_hbm, k_own), (v_hbm, v_own), (q_hbm, q_own), (g_hbm, g_own))
    outputs = (dq_hbm, dk_hbm, dv_hbm)

    def load(which):
        return pltpu.make_async_copy(inputs[which][0], inputs[which][1], load_sem.at[which])

    def store(which, head):
        return pltpu.make_async_copy(
            done.at[which, head], outputs[which].at[:, columns(head)], store_sem.at[which, head]
        )

    def forward(which, slot, sender_slot, target, head):
        return pltpu.make_async_remote_copy(
            src_ref=inputs[which][0].at[:, columns(head)],
            dst_ref=landed.at[slot, head],
            send_sem=send_sem.at[sender_slot, head],
            recv_sem=land_sem.at[slot, head],
            device_id={"group": target},
            device_id_type=MESH,
        )

    def give_back(pair, lane, target, head):
        return pltpu.make_async_remote_copy(
            src_ref=back.at[pair, head],
            dst_ref=partial.at[lane, head],
            send_sem=partial_send.at[pair, head],
            recv_sem=partial_recv.at[lane, head],
            device_id={"group": target},
            device_id_type=MESH,
        )

    def finish(which, head):
        return pltpu.make_async_remote_copy(
            src_ref=done.at[3 + which, head],
            dst_ref=outputs[which].at[:, columns(head)],
            send_sem=final_send.at[which, head],
            recv_sem=final_recv.at[which, head],
            device_id={"group": 3},
            device_id_type=MESH,
        )

    def greet(peers):
        barrier = pltpu.get_barrier_semaphore()
        for peer in peers:
            pl.semaphore_signal(barrier, inc=1, device_id={"group": peer}, device_id_type=MESH)
        pl.semaphore_wait(barrier, len(peers))

    def each_head(step):
        lax.fori_loop(0, head_count, lambda head, carry: (step(head), carry)[1], 0)

    def make_masks(first_query, query_count, key_count):
        shape = (key_count, query_count)
        key_at = lax.broadcasted_iota(jnp.int32, shape, 0)
        query_at = lax.broadcasted_iota(jnp.int32, shape, 1) + first_query
        row_at = lax.broadcasted_iota(jnp.int32, (query_count, HD), 0) + first_query
        key_span = jnp.zeros(shape, jnp.int32)
        query_span = jnp.zeros(shape, jnp.int32)
        key_end = jnp.zeros(shape, jnp.int32)
        row_end = jnp.zeros((query_count, HD), jnp.int32)
        for span in range(spans):
            start = span * span_len
            end = start + lengths[span]
            key_span = jnp.where(key_at >= start, span, key_span)
            query_span = jnp.where(query_at >= start, span, query_span)
            key_end = jnp.where(key_at >= start, end, key_end)
            row_end = jnp.where(row_at >= start, end, row_end)
        visible = (key_span <= query_span) & (key_at < key_end)
        bias[:key_count, :query_count] = jnp.where(visible, 0.0, masked_score)
        kept[:query_count, :] = jnp.where(row_at < row_end, 1.0, 0.0).astype(jnp.bfloat16)

    for which in range(4):
        load(which).start()

    def wait_loads():
        for which in range(4):
            load(which).wait()

    def low(value):
        return value.astype(jnp.bfloat16)

    @pl.when(me == 0)
    def _():
        greet((1, 2))

        def send(head):
            for which in range(2):
                forward(which, which, which, 2, head).start()
            for which in range(2):
                forward(which, which, 2 + which, 1, head).start()

        each_head(send)
        make_masks(0, rows, rows)
        wait_loads()

        def own(head):
            at = columns(head)
            dq, dk, dv = head_grads(
                q_own[:, at], g_own[:, at] * kept[:rows, :], k_own[:, at], v_own[:, at],
                bias[:rows, :rows],
            )
            done[0, head] = low(dq)
            own_sum[0, head] = dk
            own_sum[1, head] = dv
            store(0, head).start()

        each_head(own)

        def gather(head):
            give_back(0, 0, 0, head).wait_recv()
            give_back(0, 1, 0, head).wait_recv()
            for which in range(2):
                done[1 + which, head] = low(
                    own_sum[which, head]
                    + partial[0, head, which].astype(jnp.float32)
                    + partial[1, head, which].astype(jnp.float32)
                )
                store(1 + which, head).start()

        each_head(gather)

        def settle(head):
            for which in range(2):
                forward(which, which, which, 2, head).wait_send()
                forward(which, which, 2 + which, 1, head).wait_send()
            for which in range(3):
                store(which, head).wait()

        each_head(settle)

    @pl.when(me == 1)
    def _():
        greet((0, 2))

        def send(head):
            for which in range(2):
                forward(which, 2 + which, which, 2, head).start()

        each_head(send)
        make_masks(rows, rows, 2 * rows)
        wait_loads()

        def work(head):
            at = columns(head)
            for which in range(2):
                forward(which, which, 2 + which, 1, head).wait_recv()
            dq, dk, dv = head_grads(
                q_own[:, at], g_own[:, at] * kept[:rows, :],
                jnp.concatenate([landed[0, head], k_own[:, at]], axis=0),
                jnp.concatenate([landed[1, head], v_own[:, at]], axis=0),
                bias[: 2 * rows, :rows],
            )
            back[0, head, 0] = low(dk[:rows])
            back[0, head, 1] = low(dv[:rows])
            give_back(0, 0, 0, head).start()
            own_sum[0, head] = dk[rows:]
            own_sum[1, head] = dv[rows:]
            done[0, head] = low(dq)
            store(0, head).start()

        each_head(work)

        def gather(head):
            give_back(1, 0, 1, head).wait_recv()
            for which in range(2):
                done[1 + which, head] = low(
                    own_sum[which, head] + partial[0, head, which].astype(jnp.float32)
                )
                store(1 + which, head).start()

        each_head(gather)

        def settle(head):
            for which in range(2):
                forward(which, 2 + which, which, 2, head).wait_send()
            give_back(0, 0, 0, head).wait_send()
            for which in range(3):
                store(which, head).wait()

        each_head(settle)

    @pl.when(me == 2)
    def _():
        greet((0, 1, 3))
        make_masks(2 * rows, 2 * rows, 4 * rows)
        wait_loads()

        def work(head):
            at = columns(head)
            for slot in range(4):
                forward(slot % 2, slot, slot, 2, head).wait_recv()
            for which in range(4):
                forward(which, 4 + which, which, 2, head).wait_recv()
            dq, dk, dv = head_grads(
                jnp.concatenate([q_own[:, at], landed[6, head]], axis=0),
                jnp.concatenate([g_own[:, at], landed[7, head]], axis=0) * kept[...],
                jnp.concatenate(
                    [landed[0, head], landed[2, head], k_own[:, at], landed[4, head]], axis=0
                ),
                jnp.concatenate(
                    [landed[1, head], landed[3, head], v_own[:, at], landed[5, head]], axis=0
                ),
                bias[...],
            )
            for target in range(2):
                mine = slice(target * rows, (target + 1) * rows)
                back[target, head, 0] = low(dk[mine])
                back[target, head, 1] = low(dv[mine])
                give_back(target, 1 - target, target, head).start()
            for which, grad in ((1, dk), (2, dv)):
                done[which, head] = low(grad[2 * rows : 3 * rows])
                done[3 + which, head] = low(grad[3 * rows :])
            done[0, head] = low(dq[:rows])
            done[3, head] = low(dq[rows:])
            for which in range(3):
                finish(which, head).start()
                store(which, head).start()

        each_head(work)

        def settle(head):
            for target in range(2):
                give_back(target, 1 - target, target, head).wait_send()
            for which in range(3):
                finish(which, head).wait_send()
                store(which, head).wait()

        each_head(settle)

    @pl.when(me == 3)
    def _():
        greet((2,))

        def send(head):
            for which in range(4):
                forward(which, 4 + which, which, 2, head).start()

        each_head(send)
        wait_loads()

        def settle(head):
            for which in range(4):
                forward(which, 4 + which, which, 2, head).wait_send()
            for which in range(3):
                finish(which, head).wait_recv()

        each_head(settle)


def hand_over(dq, dk, dv, dq_out, dk_out, dv_out):
    dq_out[...] = dq[...]
    dk_out[...] = dk[...]
    dv_out[...] = dv[...]


def four_slices(queries, keys, values, grad_out, lengths):
    rows, features = queries.shape
    heads = features // HD
    low_type = jnp.bfloat16
    out = jax.ShapeDtypeStruct((rows, features), low_type)
    anywhere = pl.BlockSpec(memory_space=pl.ANY)
    dma = pltpu.SemaphoreType.DMA
    grads = pl.pallas_call(
        functools.partial(kernel, heads),
        out_shape=(out, out, out),
        in_specs=[pl.BlockSpec(memory_space=pltpu.SMEM)] + [anywhere] * 4,
        out_specs=(anywhere,) * 3,
        scratch_shapes=[
            pltpu.VMEM((rows, features), low_type),
            pltpu.VMEM((rows, features), low_type),
            pltpu.VMEM((rows, features), low_type),
            pltpu.VMEM((rows, features), low_type),
            pltpu.VMEM((8, heads, rows, HD), low_type),
            pltpu.VMEM((2, heads, 2, rows, HD), low_type),
            pltpu.VMEM((2, heads, 2, rows, HD), low_type),
            pltpu.VMEM((2, heads, rows, HD), jnp.float32),
            pltpu.VMEM((6, heads, rows, HD), low_type),
            pltpu.VMEM((4 * rows, 2 * rows), jnp.float32),
            pltpu.VMEM((2 * rows, HD), low_type),
            dma((4,)),
            dma((4, heads)),
            dma((8, heads)),
            dma((2, heads)),
            dma((2, heads)),
            dma((3, heads)),
            dma((3, heads)),
            dma((3, heads)),
        ],
        compiler_params=pltpu.CompilerParams(
            collective_id=0, has_side_effects=True, vmem_limit_bytes=60 * 1024 * 1024
        ),
    )(lengths, queries, keys, values, grad_out)
    return pl.pallas_call(
        hand_over,
        out_shape=(out, out, out),
        in_specs=[pl.BlockSpec(memory_space=pltpu.VMEM)] * 3,
        out_specs=(pl.BlockSpec(memory_space=pltpu.VMEM),) * 3,
    )(*grads)


def solution(mesh):
    return jax.shard_map(
        four_slices if mesh.shape["group"] == 4 else body,
        mesh=mesh,
        in_specs=(
            P(("batch", "group"), "head"),
            P(("batch", "group"), "head"),
            P(("batch", "group"), "head"),
            P(("batch", "group"), "head"),
            P("batch"),
        ),
        out_specs=(
            P(("batch", "group"), "head"),
            P(("batch", "group"), "head"),
            P(("batch", "group"), "head"),
        ),
        check_vma=False,
    )
```

```python
import functools
import math

import jax
import jax.numpy as jnp
from jax import lax
from jax.experimental import pallas as pl
from jax.experimental.pallas import tpu as pltpu
from jax.sharding import PartitionSpec as P

HD = 128


masked_score = -1e30


def passed_along(block, axis, distance):
    devices = range(lax.axis_size(axis))
    route = [((i - distance) % len(devices), i) for i in devices]
    return lax.ppermute(block, axis, route)


def lookup_length(span_ids, lengths):
    table = jnp.arange(lengths.shape[0], dtype=jnp.int32)
    return jnp.sum(jnp.where(span_ids[:, None] == table[None, :], lengths[None, :], 0), axis=1)


def heads_first(matrix, head_count):
    return matrix.reshape(matrix.shape[0], head_count, HD).transpose(1, 0, 2)


def rows_first(tensor):
    return tensor.transpose(1, 0, 2).reshape(tensor.shape[1], tensor.shape[0] * tensor.shape[2])


def body(queries, keys, values, grad_out, lengths):
    row_count, feature_count = queries.shape
    head_count = feature_count // HD
    slice_count = lax.axis_size("group")
    my_slice = lax.axis_index("group")
    score_scale = 1.0 / math.sqrt(HD)
    gathered_keys, gathered_values = (
        lax.all_gather(keys, "group", axis=0, tiled=True),
        lax.all_gather(values, "group", axis=0, tiled=True),
    )
    key_count = gathered_keys.shape[0]
    span_len = key_count // lengths.shape[0]
    key_index = jnp.arange(key_count, dtype=jnp.int32)
    key_span = key_index // span_len
    key_valid = key_index % span_len < lookup_length(key_span, lengths)
    own_index = my_slice * row_count + jnp.arange(row_count, dtype=jnp.int32)
    own_span = own_index // span_len
    own_valid = own_index % span_len < lookup_length(own_span, lengths)
    grad_kept = jnp.where(own_valid[:, None], grad_out, jnp.zeros_like(grad_out))
    top_span = jnp.max(own_span)
    query_heads = heads_first(queries, head_count)
    grad_heads = heads_first(grad_kept, head_count)
    key_heads = heads_first(gathered_keys, head_count)
    value_heads = heads_first(gathered_values, head_count)
    visible = (key_span[None, :] <= own_span[:, None]) & key_valid[None, :]

    def row_stats(head_parts):
        query_head, grad_head, key_head, value_head = head_parts
        scores = (
            jnp.einsum("rd,kd->rk", query_head, key_head, preferred_element_type=jnp.float32)
            * score_scale
        )
        scores = jnp.where(visible, scores, masked_score)
        row_max = jnp.max(scores, axis=1, keepdims=True)
        unnormed = jnp.exp(scores - row_max)
        row_sum = jnp.sum(unnormed, axis=1, keepdims=True)
        probs_low = (unnormed / row_sum).astype(jnp.bfloat16)
        attended = jnp.dot(probs_low, value_head, preferred_element_type=jnp.float32).astype(
            jnp.bfloat16
        )
        row_delta = jnp.sum(grad_head.astype(jnp.float32) * attended.astype(jnp.float32), axis=1)
        return (row_max[:, 0], row_sum[:, 0], row_delta)

    row_max, row_sum, row_delta = lax.map(
        row_stats, (query_heads, grad_heads, key_heads, value_heads)
    )

    def dense_terms(block):
        start = block * row_count
        key_block = lax.dynamic_slice_in_dim(key_heads, start, row_count, 1)
        value_block = lax.dynamic_slice_in_dim(value_heads, start, row_count, 1)
        valid_block = lax.dynamic_slice_in_dim(key_valid, start, row_count, 0)
        span_block = lax.dynamic_slice_in_dim(key_span, start, row_count, 0)
        block_mask = (span_block[None, :] <= own_span[:, None]) & valid_block[None, :]
        scores = (
            jnp.einsum("hrd,hkd->hrk", query_heads, key_block, preferred_element_type=jnp.float32)
            * score_scale
        )
        scores = jnp.where(block_mask[None], scores, masked_score)
        probs = jnp.exp(scores - row_max[:, :, None]) / row_sum[:, :, None]
        probs_low = probs.astype(jnp.bfloat16)
        prob_grad = jnp.einsum(
            "hrd,hkd->hrk", grad_heads, value_block, preferred_element_type=jnp.float32
        )
        score_grad = (probs * (prob_grad - row_delta[:, :, None])).astype(jnp.bfloat16)
        query_term = jnp.einsum(
            "hrk,hkd->hrd", score_grad, key_block, preferred_element_type=jnp.float32
        )
        key_term = rows_first(
            jnp.einsum("hrk,hrd->hkd", score_grad, query_heads, preferred_element_type=jnp.float32)
            * score_scale
        )
        value_term = rows_first(
            jnp.einsum("hrk,hrd->hkd", probs_low, grad_heads, preferred_element_type=jnp.float32)
        )
        return (query_term, key_term, value_term)

    def empty_terms(block):
        query_term = jnp.zeros((head_count, row_count, HD), jnp.float32)
        other_term = jnp.zeros((row_count, feature_count), jnp.float32)
        return (query_term, other_term, other_term)

    def block_terms(block):
        first_span = block * row_count // span_len
        return lax.cond(first_span <= top_span, dense_terms, empty_terms, block)

    query_zero = jnp.zeros((head_count, row_count, HD), jnp.float32)

    def chain_step(block_step, loop_state):
        query_grad, travel = loop_state
        block = (my_slice - block_step) % slice_count
        query_term, key_term, value_term = block_terms(block)
        travel = travel + jnp.stack([key_term, value_term])
        travel = passed_along(travel.astype(jnp.bfloat16), "group", 1).astype(travel.dtype)
        return (query_grad + query_term, travel)

    travel_zero = jnp.zeros((2, row_count, feature_count), jnp.float32)
    query_grad, travel = lax.fori_loop(0, slice_count, chain_step, (query_zero, travel_zero))
    key_grad = travel[0]
    value_grad = travel[1]
    query_low = rows_first(query_grad * score_scale).astype(jnp.bfloat16)
    return (query_low, key_grad.astype(jnp.bfloat16), value_grad.astype(jnp.bfloat16))

MESH = pl.DeviceIdType.MESH
EXP_SCALE = 1.4426950408889634 / math.sqrt(HD)
SCALE = 1.0 / math.sqrt(HD)


def dot_nt(a, b):
    return lax.dot_general(a, b, (((1,), (1,)), ((), ())), preferred_element_type=jnp.float32)


def dot_nn(a, b):
    return lax.dot_general(a, b, (((1,), (0,)), ((), ())), preferred_element_type=jnp.float32)


def dot_tn(a, b):
    return lax.dot_general(a, b, (((0,), (0,)), ((), ())), preferred_element_type=jnp.float32)


def head_probs(query, key, bias):
    scores = dot_nt(key, query) * EXP_SCALE + bias
    top = jnp.max(scores, axis=0, keepdims=True)
    unnormed = jnp.exp2(scores - top)
    total = jnp.sum(unnormed, axis=0, keepdims=True)
    return unnormed * (1.0 / total)


def head_score_grad(probs, grad, value):
    prob_grad = dot_nt(value, grad)
    delta = jnp.sum(probs * prob_grad, axis=0, keepdims=True)
    return (probs * (prob_grad - delta)).astype(jnp.bfloat16)


def columns(head):
    return pl.ds(pl.multiple_of(head * HD, HD), HD)


def kernel(
    head_count, lengths, q_hbm, k_hbm, v_hbm, g_hbm, dq_out_ref, dk_out_ref, dv_out_ref,
    q_own, k_own, v_own, g_own, landed, back, partial, own_sum, done, bias, kept,
    load_sem, send_sem, land_sem, partial_send, partial_recv, final_send, final_recv,
):
    me = lax.axis_index("group")
    rows = q_hbm.shape[0]
    spans = lengths.shape[0]
    span_len = 4 * rows // spans
    inputs = ((k_hbm, k_own), (v_hbm, v_own), (q_hbm, q_own), (g_hbm, g_own))
    outputs = (dq_out_ref, dk_out_ref, dv_out_ref)

    def load(which):
        return pltpu.make_async_copy(inputs[which][0], inputs[which][1], load_sem.at[which])

    def forward(which, slot, sender_slot, target, head):
        return pltpu.make_async_remote_copy(
            src_ref=inputs[which][0].at[:, columns(head)],
            dst_ref=landed.at[slot, head],
            send_sem=send_sem.at[sender_slot, head],
            recv_sem=land_sem.at[slot, head],
            device_id={"group": target},
            device_id_type=MESH,
        )

    def give_back(pair, lane, which, target, head):
        return pltpu.make_async_remote_copy(
            src_ref=back.at[pair, which, head],
            dst_ref=partial.at[lane, which, head],
            send_sem=partial_send.at[pair, which, head],
            recv_sem=partial_recv.at[lane, which, head],
            device_id={"group": target},
            device_id_type=MESH,
        )

    def finish(which, head):
        return pltpu.make_async_remote_copy(
            src_ref=done.at[which, head],
            dst_ref=outputs[which].at[:, columns(head)],
            send_sem=final_send.at[which, head],
            recv_sem=final_recv.at[which, head],
            device_id={"group": 3},
            device_id_type=MESH,
        )

    def greet(peers):
        barrier = pltpu.get_barrier_semaphore()
        for peer in peers:
            pl.semaphore_signal(barrier, inc=1, device_id={"group": peer}, device_id_type=MESH)
        pl.semaphore_wait(barrier, len(peers))

    def each_head(step):
        lax.fori_loop(0, head_count, lambda head, carry: (step(head), carry)[1], 0)

    def make_masks(first_query, query_count, key_count):
        shape = (key_count, query_count)
        key_at = lax.broadcasted_iota(jnp.int32, shape, 0)
        query_at = lax.broadcasted_iota(jnp.int32, shape, 1) + first_query
        row_at = lax.broadcasted_iota(jnp.int32, (query_count, HD), 0) + first_query
        key_span = jnp.zeros(shape, jnp.int32)
        query_span = jnp.zeros(shape, jnp.int32)
        key_end = jnp.zeros(shape, jnp.int32)
        row_end = jnp.zeros((query_count, HD), jnp.int32)
        for span in range(spans):
            start = span * span_len
            end = start + lengths[span]
            key_span = jnp.where(key_at >= start, span, key_span)
            query_span = jnp.where(query_at >= start, span, query_span)
            key_end = jnp.where(key_at >= start, end, key_end)
            row_end = jnp.where(row_at >= start, end, row_end)
        visible = (key_span <= query_span) & (key_at < key_end)
        bias[:key_count, :query_count] = jnp.where(visible, 0.0, masked_score)
        kept[:query_count, :] = jnp.where(row_at < row_end, 1.0, 0.0).astype(jnp.bfloat16)

    for which in range(4):
        load(which).start()

    def wait_loads():
        for which in range(4):
            load(which).wait()

    def low(value):
        return value.astype(jnp.bfloat16)

    @pl.when(me == 0)
    def _():
        greet((1, 2))

        def send(head):
            for which in range(2):
                forward(which, which, which, 2, head).start()
            for which in range(2):
                forward(which, which, 2 + which, 1, head).start()

        each_head(send)
        make_masks(0, rows, rows)
        wait_loads()

        def own(head):
            at = columns(head)
            query, key = q_own[:, at], k_own[:, at]
            grad = g_own[:, at] * kept[:rows, :]
            probs = head_probs(query, key, bias[:rows, :rows])
            own_sum[1, head] = dot_nn(low(probs), grad)
            score_grad = head_score_grad(probs, grad, v_own[:, at])
            own_sum[0, head] = dot_nn(score_grad, query) * SCALE
            dq_out_ref[:, at] = low(dot_tn(score_grad, key) * SCALE)

        each_head(own)

        def gather(head):
            at = columns(head)
            for which in (1, 0):
                give_back(0, 0, which, 0, head).wait_recv()
                give_back(0, 1, which, 0, head).wait_recv()
                outputs[1 + which][:, at] = low(
                    own_sum[which, head]
                    + partial[0, which, head].astype(jnp.float32)
                    + partial[1, which, head].astype(jnp.float32)
                )

        each_head(gather)

        def settle(head):
            for which in range(2):
                forward(which, which, which, 2, head).wait_send()
                forward(which, which, 2 + which, 1, head).wait_send()

        each_head(settle)

    @pl.when(me == 1)
    def _():
        greet((0, 2))

        def send(head):
            for which in range(2):
                forward(which, 2 + which, which, 2, head).start()

        each_head(send)
        make_masks(rows, rows, 2 * rows)
        wait_loads()

        def work(head):
            at = columns(head)
            query = q_own[:, at]
            grad = g_own[:, at] * kept[:rows, :]
            forward(0, 0, 2, 1, head).wait_recv()
            key = jnp.concatenate([landed[0, head], k_own[:, at]], axis=0)
            probs = head_probs(query, key, bias[: 2 * rows, :rows])
            dv = dot_nn(low(probs), grad)
            back[0, 1, head] = low(dv[:rows])
            give_back(0, 0, 1, 0, head).start()
            own_sum[1, head] = dv[rows:]
            forward(1, 1, 3, 1, head).wait_recv()
            value = jnp.concatenate([landed[1, head], v_own[:, at]], axis=0)
            score_grad = head_score_grad(probs, grad, value)
            dk = dot_nn(score_grad, query) * SCALE
            back[0, 0, head] = low(dk[:rows])
            give_back(0, 0, 0, 0, head).start()
            own_sum[0, head] = dk[rows:]
            dq_out_ref[:, at] = low(dot_tn(score_grad, key) * SCALE)

        each_head(work)

        def gather(head):
            at = columns(head)
            for which in (1, 0):
                give_back(1, 0, which, 1, head).wait_recv()
                outputs[1 + which][:, at] = low(
                    own_sum[which, head] + partial[0, which, head].astype(jnp.float32)
                )

        each_head(gather)

        def settle(head):
            for which in range(2):
                forward(which, 2 + which, which, 2, head).wait_send()
            for which in range(2):
                give_back(0, 0, which, 0, head).wait_send()

        each_head(settle)

    @pl.when(me == 2)
    def _():
        greet((0, 1, 3))
        make_masks(2 * rows, 2 * rows, 4 * rows)
        wait_loads()

        def work(head):
            at = columns(head)

            def arrive(which, slot):
                forward(which, slot, which, 2, head).wait_recv()

            def give(which, grad_sum):
                for target in range(2):
                    mine = slice(target * rows, (target + 1) * rows)
                    back[target, which, head] = low(grad_sum[mine])
                    give_back(target, 1 - target, which, target, head).start()
                done[1 + which, head] = low(grad_sum[3 * rows :])
                finish(1 + which, head).start()
                outputs[1 + which][:, at] = low(grad_sum[2 * rows : 3 * rows])

            arrive(2, 6)
            arrive(3, 7)
            arrive(0, 4)
            arrive(0, 0)
            arrive(0, 2)
            query = jnp.concatenate([q_own[:, at], landed[6, head]], axis=0)
            grad = jnp.concatenate([g_own[:, at], landed[7, head]], axis=0) * kept[...]
            key = jnp.concatenate(
                [landed[0, head], landed[2, head], k_own[:, at], landed[4, head]], axis=0
            )
            probs = head_probs(query, key, bias[...])
            give(1, dot_nn(low(probs), grad))
            arrive(1, 5)
            arrive(1, 1)
            arrive(1, 3)
            value = jnp.concatenate(
                [landed[1, head], landed[3, head], v_own[:, at], landed[5, head]], axis=0
            )
            score_grad = head_score_grad(probs, grad, value)
            give(0, dot_nn(score_grad, query) * SCALE)
            dq = dot_tn(score_grad, key) * SCALE
            dq_out_ref[:, at] = low(dq[:rows])
            done[0, head] = low(dq[rows:])
            finish(0, head).start()

        each_head(work)

        def settle(head):
            for target in range(2):
                for which in range(2):
                    give_back(target, 1 - target, which, target, head).wait_send()
            for which in range(3):
                finish(which, head).wait_send()

        each_head(settle)

    @pl.when(me == 3)
    def _():
        greet((2,))

        def send(head):
            for which in (0, 2, 3, 1):
                forward(which, 4 + which, which, 2, head).start()

        each_head(send)
        wait_loads()

        def settle(head):
            for which in range(4):
                forward(which, 4 + which, which, 2, head).wait_send()
            for which in range(3):
                finish(which, head).wait_recv()

        each_head(settle)


def four_slices(queries, keys, values, grad_out, lengths):
    rows, features = queries.shape
    heads = features // HD
    low_type = jnp.bfloat16
    out = jax.ShapeDtypeStruct((rows, features), low_type)
    anywhere = pl.BlockSpec(memory_space=pl.ANY)
    dma = pltpu.SemaphoreType.DMA
    return pl.pallas_call(
        functools.partial(kernel, heads),
        out_shape=(pltpu.VMEM((rows, features), low_type),) * 3,
        in_specs=[pl.BlockSpec(memory_space=pltpu.SMEM)] + [anywhere] * 4,
        out_specs=(pl.BlockSpec(memory_space=pltpu.VMEM),) * 3,
        scratch_shapes=[
            pltpu.VMEM((rows, features), low_type),
            pltpu.VMEM((rows, features), low_type),
            pltpu.VMEM((rows, features), low_type),
            pltpu.VMEM((rows, features), low_type),
            pltpu.VMEM((8, heads, rows, HD), low_type),
            pltpu.VMEM((2, 2, heads, rows, HD), low_type),
            pltpu.VMEM((2, 2, heads, rows, HD), low_type),
            pltpu.VMEM((2, heads, rows, HD), jnp.float32),
            pltpu.VMEM((3, heads, rows, HD), low_type),
            pltpu.VMEM((4 * rows, 2 * rows), jnp.float32),
            pltpu.VMEM((2 * rows, HD), low_type),
            dma((4,)),
            dma((4, heads)),
            dma((8, heads)),
            dma((2, 2, heads)),
            dma((2, 2, heads)),
            dma((3, heads)),
            dma((3, heads)),
        ],
        compiler_params=pltpu.CompilerParams(
            collective_id=0, has_side_effects=True, vmem_limit_bytes=60 * 1024 * 1024
        ),
    )(lengths, queries, keys, values, grad_out)


def solution(mesh):
    return jax.shard_map(
        four_slices if mesh.shape["group"] == 4 else body,
        mesh=mesh,
        in_specs=(
            P(("batch", "group"), "head"),
            P(("batch", "group"), "head"),
            P(("batch", "group"), "head"),
            P(("batch", "group"), "head"),
            P("batch"),
        ),
        out_specs=(
            P(("batch", "group"), "head"),
            P(("batch", "group"), "head"),
            P(("batch", "group"), "head"),
        ),
        check_vma=False,
    )
```

```python
import functools
import math

import jax
import jax.numpy as jnp
from jax import lax
from jax.experimental import pallas as pl
from jax.experimental.pallas import tpu as pltpu
from jax.sharding import PartitionSpec as P

HD = 128


masked_score = -1e30


def passed_along(block, axis, distance):
    devices = range(lax.axis_size(axis))
    route = [((i - distance) % len(devices), i) for i in devices]
    return lax.ppermute(block, axis, route)


def lookup_length(span_ids, lengths):
    table = jnp.arange(lengths.shape[0], dtype=jnp.int32)
    return jnp.sum(jnp.where(span_ids[:, None] == table[None, :], lengths[None, :], 0), axis=1)


def heads_first(matrix, head_count):
    return matrix.reshape(matrix.shape[0], head_count, HD).transpose(1, 0, 2)


def rows_first(tensor):
    return tensor.transpose(1, 0, 2).reshape(tensor.shape[1], tensor.shape[0] * tensor.shape[2])


def body(queries, keys, values, grad_out, lengths):
    row_count, feature_count = queries.shape
    head_count = feature_count // HD
    slice_count = lax.axis_size("group")
    my_slice = lax.axis_index("group")
    score_scale = 1.0 / math.sqrt(HD)
    gathered_keys, gathered_values = (
        lax.all_gather(keys, "group", axis=0, tiled=True),
        lax.all_gather(values, "group", axis=0, tiled=True),
    )
    key_count = gathered_keys.shape[0]
    span_len = key_count // lengths.shape[0]
    key_index = jnp.arange(key_count, dtype=jnp.int32)
    key_span = key_index // span_len
    key_valid = key_index % span_len < lookup_length(key_span, lengths)
    own_index = my_slice * row_count + jnp.arange(row_count, dtype=jnp.int32)
    own_span = own_index // span_len
    own_valid = own_index % span_len < lookup_length(own_span, lengths)
    grad_kept = jnp.where(own_valid[:, None], grad_out, jnp.zeros_like(grad_out))
    top_span = jnp.max(own_span)
    query_heads = heads_first(queries, head_count)
    grad_heads = heads_first(grad_kept, head_count)
    key_heads = heads_first(gathered_keys, head_count)
    value_heads = heads_first(gathered_values, head_count)
    visible = (key_span[None, :] <= own_span[:, None]) & key_valid[None, :]

    def row_stats(head_parts):
        query_head, grad_head, key_head, value_head = head_parts
        scores = (
            jnp.einsum("rd,kd->rk", query_head, key_head, preferred_element_type=jnp.float32)
            * score_scale
        )
        scores = jnp.where(visible, scores, masked_score)
        row_max = jnp.max(scores, axis=1, keepdims=True)
        unnormed = jnp.exp(scores - row_max)
        row_sum = jnp.sum(unnormed, axis=1, keepdims=True)
        probs_low = (unnormed / row_sum).astype(jnp.bfloat16)
        attended = jnp.dot(probs_low, value_head, preferred_element_type=jnp.float32).astype(
            jnp.bfloat16
        )
        row_delta = jnp.sum(grad_head.astype(jnp.float32) * attended.astype(jnp.float32), axis=1)
        return (row_max[:, 0], row_sum[:, 0], row_delta)

    row_max, row_sum, row_delta = lax.map(
        row_stats, (query_heads, grad_heads, key_heads, value_heads)
    )

    def dense_terms(block):
        start = block * row_count
        key_block = lax.dynamic_slice_in_dim(key_heads, start, row_count, 1)
        value_block = lax.dynamic_slice_in_dim(value_heads, start, row_count, 1)
        valid_block = lax.dynamic_slice_in_dim(key_valid, start, row_count, 0)
        span_block = lax.dynamic_slice_in_dim(key_span, start, row_count, 0)
        block_mask = (span_block[None, :] <= own_span[:, None]) & valid_block[None, :]
        scores = (
            jnp.einsum("hrd,hkd->hrk", query_heads, key_block, preferred_element_type=jnp.float32)
            * score_scale
        )
        scores = jnp.where(block_mask[None], scores, masked_score)
        probs = jnp.exp(scores - row_max[:, :, None]) / row_sum[:, :, None]
        probs_low = probs.astype(jnp.bfloat16)
        prob_grad = jnp.einsum(
            "hrd,hkd->hrk", grad_heads, value_block, preferred_element_type=jnp.float32
        )
        score_grad = (probs * (prob_grad - row_delta[:, :, None])).astype(jnp.bfloat16)
        query_term = jnp.einsum(
            "hrk,hkd->hrd", score_grad, key_block, preferred_element_type=jnp.float32
        )
        key_term = rows_first(
            jnp.einsum("hrk,hrd->hkd", score_grad, query_heads, preferred_element_type=jnp.float32)
            * score_scale
        )
        value_term = rows_first(
            jnp.einsum("hrk,hrd->hkd", probs_low, grad_heads, preferred_element_type=jnp.float32)
        )
        return (query_term, key_term, value_term)

    def empty_terms(block):
        query_term = jnp.zeros((head_count, row_count, HD), jnp.float32)
        other_term = jnp.zeros((row_count, feature_count), jnp.float32)
        return (query_term, other_term, other_term)

    def block_terms(block):
        first_span = block * row_count // span_len
        return lax.cond(first_span <= top_span, dense_terms, empty_terms, block)

    query_zero = jnp.zeros((head_count, row_count, HD), jnp.float32)

    def chain_step(block_step, loop_state):
        query_grad, travel = loop_state
        block = (my_slice - block_step) % slice_count
        query_term, key_term, value_term = block_terms(block)
        travel = travel + jnp.stack([key_term, value_term])
        travel = passed_along(travel.astype(jnp.bfloat16), "group", 1).astype(travel.dtype)
        return (query_grad + query_term, travel)

    travel_zero = jnp.zeros((2, row_count, feature_count), jnp.float32)
    query_grad, travel = lax.fori_loop(0, slice_count, chain_step, (query_zero, travel_zero))
    key_grad = travel[0]
    value_grad = travel[1]
    query_low = rows_first(query_grad * score_scale).astype(jnp.bfloat16)
    return (query_low, key_grad.astype(jnp.bfloat16), value_grad.astype(jnp.bfloat16))

MESH = pl.DeviceIdType.MESH
EXP_SCALE = 1.4426950408889634 / math.sqrt(HD)
SCALE = 1.0 / math.sqrt(HD)


def dot_nt(a, b):
    return lax.dot_general(a, b, (((1,), (1,)), ((), ())), preferred_element_type=jnp.float32)


def dot_nn(a, b):
    return lax.dot_general(a, b, (((1,), (0,)), ((), ())), preferred_element_type=jnp.float32)


def dot_tn(a, b):
    return lax.dot_general(a, b, (((0,), (0,)), ((), ())), preferred_element_type=jnp.float32)


def head_probs(query, key, bias):
    scores = dot_nt(key, query) * EXP_SCALE + bias
    top = jnp.max(scores, axis=0, keepdims=True)
    unnormed = jnp.exp2(scores - top)
    total = jnp.sum(unnormed, axis=0, keepdims=True)
    return unnormed * (1.0 / total)


def head_score_grad(probs, grad, value):
    prob_grad = dot_nt(value, grad)
    delta = jnp.sum(probs * prob_grad, axis=0, keepdims=True)
    return (probs * (prob_grad - delta)).astype(jnp.bfloat16)


def columns(head):
    return pl.ds(pl.multiple_of(head * HD, HD), HD)


def kernel(
    head_count, lengths, q_hbm, k_hbm, v_hbm, g_hbm, dq_out_ref, dk_out_ref, dv_out_ref,
    q_own, k_own, v_own, g_own, landed, back, partial, own_sum, done, bias, kept,
    load_sem, send_sem, land_sem, partial_send, partial_recv, final_send, final_recv,
):
    me = lax.axis_index("group")
    rows = q_hbm.shape[0]
    spans = lengths.shape[0]
    span_len = 4 * rows // spans
    inputs = ((k_hbm, k_own), (v_hbm, v_own), (q_hbm, q_own), (g_hbm, g_own))
    outputs = (dq_out_ref, dk_out_ref, dv_out_ref)

    def load(which):
        return pltpu.make_async_copy(inputs[which][0], inputs[which][1], load_sem.at[which])

    def forward(which, slot, sender_slot, target, head):
        return pltpu.make_async_remote_copy(
            src_ref=inputs[which][0].at[:, columns(head)],
            dst_ref=landed.at[slot, head],
            send_sem=send_sem.at[sender_slot, head],
            recv_sem=land_sem.at[slot, head],
            device_id={"group": target},
            device_id_type=MESH,
        )

    def give_back(pair, lane, which, target, head):
        return pltpu.make_async_remote_copy(
            src_ref=back.at[pair, which, head],
            dst_ref=partial.at[lane, which, head],
            send_sem=partial_send.at[pair, which, head],
            recv_sem=partial_recv.at[lane, which, head],
            device_id={"group": target},
            device_id_type=MESH,
        )

    def finish(which, head):
        return pltpu.make_async_remote_copy(
            src_ref=done.at[which, head],
            dst_ref=outputs[which].at[:, columns(head)],
            send_sem=final_send.at[which, head],
            recv_sem=final_recv.at[which, head],
            device_id={"group": 3},
            device_id_type=MESH,
        )

    def greet(peers):
        barrier = pltpu.get_barrier_semaphore()
        for peer in peers:
            pl.semaphore_signal(barrier, inc=1, device_id={"group": peer}, device_id_type=MESH)
        pl.semaphore_wait(barrier, len(peers))

    def each_head(step):
        lax.fori_loop(0, head_count, lambda head, carry: (step(head), carry)[1], 0)

    def make_masks(first_query, query_count, key_count):
        shape = (key_count, query_count)
        key_at = lax.broadcasted_iota(jnp.int32, shape, 0)
        query_at = lax.broadcasted_iota(jnp.int32, shape, 1) + first_query
        row_at = lax.broadcasted_iota(jnp.int32, (query_count, HD), 0) + first_query
        key_span = jnp.zeros(shape, jnp.int32)
        query_span = jnp.zeros(shape, jnp.int32)
        key_end = jnp.zeros(shape, jnp.int32)
        row_end = jnp.zeros((query_count, HD), jnp.int32)
        for span in range(spans):
            start = span * span_len
            end = start + lengths[span]
            key_span = jnp.where(key_at >= start, span, key_span)
            query_span = jnp.where(query_at >= start, span, query_span)
            key_end = jnp.where(key_at >= start, end, key_end)
            row_end = jnp.where(row_at >= start, end, row_end)
        visible = (key_span <= query_span) & (key_at < key_end)
        bias[:key_count, :query_count] = jnp.where(visible, 0.0, masked_score)
        kept[:query_count, :] = jnp.where(row_at < row_end, 1.0, 0.0).astype(jnp.bfloat16)

    for which in range(4):
        load(which).start()

    def wait_loads():
        for which in range(4):
            load(which).wait()

    def low(value):
        return value.astype(jnp.bfloat16)

    @pl.when(me == 0)
    def _():
        greet((1, 2))

        def send(head):
            for which in range(2):
                forward(which, which, 2 + which, 1, head).start()
                forward(which, which, which, 2, head).start()

        each_head(send)
        make_masks(0, rows, rows)
        wait_loads()

        def own(head):
            at = columns(head)
            query, key = q_own[:, at], k_own[:, at]
            grad = g_own[:, at] * kept[:rows, :]
            probs = head_probs(query, key, bias[:rows, :rows])
            own_sum[1, head] = dot_nn(low(probs), grad)
            score_grad = head_score_grad(probs, grad, v_own[:, at])
            own_sum[0, head] = dot_nn(score_grad, query) * SCALE
            dq_out_ref[:, at] = low(dot_tn(score_grad, key) * SCALE)

        each_head(own)

        def gather(head):
            at = columns(head)
            for which in (1, 0):
                give_back(0, 0, which, 0, head).wait_recv()
                give_back(0, 1, which, 0, head).wait_recv()
                outputs[1 + which][:, at] = low(
                    own_sum[which, head]
                    + partial[0, which, head].astype(jnp.float32)
                    + partial[1, which, head].astype(jnp.float32)
                )

        each_head(gather)

        def settle(head):
            for which in range(2):
                forward(which, which, which, 2, head).wait_send()
                forward(which, which, 2 + which, 1, head).wait_send()

        each_head(settle)

    @pl.when(me == 1)
    def _():
        greet((0, 2))

        def send(head):
            for which in range(2):
                forward(which, 2 + which, which, 2, head).start()

        each_head(send)
        make_masks(rows, rows, 2 * rows)
        wait_loads()

        def work(head):
            at = columns(head)
            query = q_own[:, at]
            grad = g_own[:, at] * kept[:rows, :]
            forward(0, 0, 2, 1, head).wait_recv()
            key = jnp.concatenate([landed[0, head], k_own[:, at]], axis=0)
            probs = head_probs(query, key, bias[: 2 * rows, :rows])
            dv = dot_nn(low(probs), grad)
            back[0, 1, head] = low(dv[:rows])
            give_back(0, 0, 1, 0, head).start()
            own_sum[1, head] = dv[rows:]
            forward(1, 1, 3, 1, head).wait_recv()
            value = jnp.concatenate([landed[1, head], v_own[:, at]], axis=0)
            score_grad = head_score_grad(probs, grad, value)
            dk = dot_nn(score_grad, query) * SCALE
            back[0, 0, head] = low(dk[:rows])
            give_back(0, 0, 0, 0, head).start()
            own_sum[0, head] = dk[rows:]
            dq_out_ref[:, at] = low(dot_tn(score_grad, key) * SCALE)

        each_head(work)

        def gather(head):
            at = columns(head)
            for which in (1, 0):
                give_back(1, 0, which, 1, head).wait_recv()
                outputs[1 + which][:, at] = low(
                    own_sum[which, head] + partial[0, which, head].astype(jnp.float32)
                )

        each_head(gather)

        def settle(head):
            for which in range(2):
                forward(which, 2 + which, which, 2, head).wait_send()
            for which in range(2):
                give_back(0, 0, which, 0, head).wait_send()

        each_head(settle)

    @pl.when(me == 2)
    def _():
        greet((0, 1, 3))
        make_masks(2 * rows, 2 * rows, 4 * rows)
        wait_loads()

        def work(head):
            at = columns(head)

            def arrive(which, slot):
                forward(which, slot, which, 2, head).wait_recv()

            def give(which, grad_sum):
                for target in range(2):
                    mine = slice(target * rows, (target + 1) * rows)
                    back[target, which, head] = low(grad_sum[mine])
                    give_back(target, 1 - target, which, target, head).start()
                done[1 + which, head] = low(grad_sum[3 * rows :])
                finish(1 + which, head).start()
                outputs[1 + which][:, at] = low(grad_sum[2 * rows : 3 * rows])

            arrive(2, 6)
            arrive(3, 7)
            arrive(0, 4)
            arrive(0, 0)
            arrive(0, 2)
            query = jnp.concatenate([q_own[:, at], landed[6, head]], axis=0)
            grad = jnp.concatenate([g_own[:, at], landed[7, head]], axis=0) * kept[...]
            key = jnp.concatenate(
                [landed[0, head], landed[2, head], k_own[:, at], landed[4, head]], axis=0
            )
            probs = head_probs(query, key, bias[...])
            give(1, dot_nn(low(probs), grad))
            arrive(1, 5)
            arrive(1, 1)
            arrive(1, 3)
            value = jnp.concatenate(
                [landed[1, head], landed[3, head], v_own[:, at], landed[5, head]], axis=0
            )
            score_grad = head_score_grad(probs, grad, value)
            give(0, dot_nn(score_grad, query) * SCALE)
            dq = dot_tn(score_grad, key) * SCALE
            dq_out_ref[:, at] = low(dq[:rows])
            done[0, head] = low(dq[rows:])
            finish(0, head).start()

        each_head(work)

        def settle(head):
            for target in range(2):
                for which in range(2):
                    give_back(target, 1 - target, which, target, head).wait_send()
            for which in range(3):
                finish(which, head).wait_send()

        each_head(settle)

    @pl.when(me == 3)
    def _():
        greet((2,))

        def send(head):
            for which in (0, 2, 3, 1):
                forward(which, 4 + which, which, 2, head).start()

        each_head(send)
        wait_loads()

        def settle(head):
            for which in range(4):
                forward(which, 4 + which, which, 2, head).wait_send()
            for which in range(3):
                finish(which, head).wait_recv()

        each_head(settle)


def four_slices(queries, keys, values, grad_out, lengths):
    rows, features = queries.shape
    heads = features // HD
    low_type = jnp.bfloat16
    out = jax.ShapeDtypeStruct((rows, features), low_type)
    anywhere = pl.BlockSpec(memory_space=pl.ANY)
    dma = pltpu.SemaphoreType.DMA
    return pl.pallas_call(
        functools.partial(kernel, heads),
        out_shape=(pltpu.VMEM((rows, features), low_type),) * 3,
        in_specs=[pl.BlockSpec(memory_space=pltpu.SMEM)] + [anywhere] * 4,
        out_specs=(pl.BlockSpec(memory_space=pltpu.VMEM),) * 3,
        scratch_shapes=[
            pltpu.VMEM((rows, features), low_type),
            pltpu.VMEM((rows, features), low_type),
            pltpu.VMEM((rows, features), low_type),
            pltpu.VMEM((rows, features), low_type),
            pltpu.VMEM((8, heads, rows, HD), low_type),
            pltpu.VMEM((2, 2, heads, rows, HD), low_type),
            pltpu.VMEM((2, 2, heads, rows, HD), low_type),
            pltpu.VMEM((2, heads, rows, HD), jnp.float32),
            pltpu.VMEM((3, heads, rows, HD), low_type),
            pltpu.VMEM((4 * rows, 2 * rows), jnp.float32),
            pltpu.VMEM((2 * rows, HD), low_type),
            dma((4,)),
            dma((4, heads)),
            dma((8, heads)),
            dma((2, 2, heads)),
            dma((2, 2, heads)),
            dma((3, heads)),
            dma((3, heads)),
        ],
        compiler_params=pltpu.CompilerParams(
            collective_id=0, has_side_effects=True, vmem_limit_bytes=60 * 1024 * 1024
        ),
    )(lengths, queries, keys, values, grad_out)


def solution(mesh):
    return jax.shard_map(
        four_slices if mesh.shape["group"] == 4 else body,
        mesh=mesh,
        in_specs=(
            P(("batch", "group"), "head"),
            P(("batch", "group"), "head"),
            P(("batch", "group"), "head"),
            P(("batch", "group"), "head"),
            P("batch"),
        ),
        out_specs=(
            P(("batch", "group"), "head"),
            P(("batch", "group"), "head"),
            P(("batch", "group"), "head"),
        ),
        check_vma=False,
    )
```

```python
import functools
import math

import jax
import jax.numpy as jnp
from jax import lax
from jax.experimental import pallas as pl
from jax.experimental.pallas import tpu as pltpu
from jax.sharding import PartitionSpec as P

HD = 128


masked_score = -1e30


def passed_along(block, axis, distance):
    devices = range(lax.axis_size(axis))
    route = [((i - distance) % len(devices), i) for i in devices]
    return lax.ppermute(block, axis, route)


def lookup_length(span_ids, lengths):
    table = jnp.arange(lengths.shape[0], dtype=jnp.int32)
    return jnp.sum(jnp.where(span_ids[:, None] == table[None, :], lengths[None, :], 0), axis=1)


def heads_first(matrix, head_count):
    return matrix.reshape(matrix.shape[0], head_count, HD).transpose(1, 0, 2)


def rows_first(tensor):
    return tensor.transpose(1, 0, 2).reshape(tensor.shape[1], tensor.shape[0] * tensor.shape[2])


def body(queries, keys, values, grad_out, lengths):
    row_count, feature_count = queries.shape
    head_count = feature_count // HD
    slice_count = lax.axis_size("group")
    my_slice = lax.axis_index("group")
    score_scale = 1.0 / math.sqrt(HD)
    gathered_keys, gathered_values = (
        lax.all_gather(keys, "group", axis=0, tiled=True),
        lax.all_gather(values, "group", axis=0, tiled=True),
    )
    key_count = gathered_keys.shape[0]
    span_len = key_count // lengths.shape[0]
    key_index = jnp.arange(key_count, dtype=jnp.int32)
    key_span = key_index // span_len
    key_valid = key_index % span_len < lookup_length(key_span, lengths)
    own_index = my_slice * row_count + jnp.arange(row_count, dtype=jnp.int32)
    own_span = own_index // span_len
    own_valid = own_index % span_len < lookup_length(own_span, lengths)
    grad_kept = jnp.where(own_valid[:, None], grad_out, jnp.zeros_like(grad_out))
    top_span = jnp.max(own_span)
    query_heads = heads_first(queries, head_count)
    grad_heads = heads_first(grad_kept, head_count)
    key_heads = heads_first(gathered_keys, head_count)
    value_heads = heads_first(gathered_values, head_count)
    visible = (key_span[None, :] <= own_span[:, None]) & key_valid[None, :]

    def row_stats(head_parts):
        query_head, grad_head, key_head, value_head = head_parts
        scores = (
            jnp.einsum("rd,kd->rk", query_head, key_head, preferred_element_type=jnp.float32)
            * score_scale
        )
        scores = jnp.where(visible, scores, masked_score)
        row_max = jnp.max(scores, axis=1, keepdims=True)
        unnormed = jnp.exp(scores - row_max)
        row_sum = jnp.sum(unnormed, axis=1, keepdims=True)
        probs_low = (unnormed / row_sum).astype(jnp.bfloat16)
        attended = jnp.dot(probs_low, value_head, preferred_element_type=jnp.float32).astype(
            jnp.bfloat16
        )
        row_delta = jnp.sum(grad_head.astype(jnp.float32) * attended.astype(jnp.float32), axis=1)
        return (row_max[:, 0], row_sum[:, 0], row_delta)

    row_max, row_sum, row_delta = lax.map(
        row_stats, (query_heads, grad_heads, key_heads, value_heads)
    )

    def dense_terms(block):
        start = block * row_count
        key_block = lax.dynamic_slice_in_dim(key_heads, start, row_count, 1)
        value_block = lax.dynamic_slice_in_dim(value_heads, start, row_count, 1)
        valid_block = lax.dynamic_slice_in_dim(key_valid, start, row_count, 0)
        span_block = lax.dynamic_slice_in_dim(key_span, start, row_count, 0)
        block_mask = (span_block[None, :] <= own_span[:, None]) & valid_block[None, :]
        scores = (
            jnp.einsum("hrd,hkd->hrk", query_heads, key_block, preferred_element_type=jnp.float32)
            * score_scale
        )
        scores = jnp.where(block_mask[None], scores, masked_score)
        probs = jnp.exp(scores - row_max[:, :, None]) / row_sum[:, :, None]
        probs_low = probs.astype(jnp.bfloat16)
        prob_grad = jnp.einsum(
            "hrd,hkd->hrk", grad_heads, value_block, preferred_element_type=jnp.float32
        )
        score_grad = (probs * (prob_grad - row_delta[:, :, None])).astype(jnp.bfloat16)
        query_term = jnp.einsum(
            "hrk,hkd->hrd", score_grad, key_block, preferred_element_type=jnp.float32
        )
        key_term = rows_first(
            jnp.einsum("hrk,hrd->hkd", score_grad, query_heads, preferred_element_type=jnp.float32)
            * score_scale
        )
        value_term = rows_first(
            jnp.einsum("hrk,hrd->hkd", probs_low, grad_heads, preferred_element_type=jnp.float32)
        )
        return (query_term, key_term, value_term)

    def empty_terms(block):
        query_term = jnp.zeros((head_count, row_count, HD), jnp.float32)
        other_term = jnp.zeros((row_count, feature_count), jnp.float32)
        return (query_term, other_term, other_term)

    def block_terms(block):
        first_span = block * row_count // span_len
        return lax.cond(first_span <= top_span, dense_terms, empty_terms, block)

    query_zero = jnp.zeros((head_count, row_count, HD), jnp.float32)

    def chain_step(block_step, loop_state):
        query_grad, travel = loop_state
        block = (my_slice - block_step) % slice_count
        query_term, key_term, value_term = block_terms(block)
        travel = travel + jnp.stack([key_term, value_term])
        travel = passed_along(travel.astype(jnp.bfloat16), "group", 1).astype(travel.dtype)
        return (query_grad + query_term, travel)

    travel_zero = jnp.zeros((2, row_count, feature_count), jnp.float32)
    query_grad, travel = lax.fori_loop(0, slice_count, chain_step, (query_zero, travel_zero))
    key_grad = travel[0]
    value_grad = travel[1]
    query_low = rows_first(query_grad * score_scale).astype(jnp.bfloat16)
    return (query_low, key_grad.astype(jnp.bfloat16), value_grad.astype(jnp.bfloat16))

MESH = pl.DeviceIdType.MESH
EXP_SCALE = 1.4426950408889634 / math.sqrt(HD)
SCALE = 1.0 / math.sqrt(HD)


def dot_nt(a, b):
    return lax.dot_general(a, b, (((1,), (1,)), ((), ())), preferred_element_type=jnp.float32)


def dot_nn(a, b):
    return lax.dot_general(a, b, (((1,), (0,)), ((), ())), preferred_element_type=jnp.float32)


def dot_tn(a, b):
    return lax.dot_general(a, b, (((0,), (0,)), ((), ())), preferred_element_type=jnp.float32)


def head_probs(query, key, bias):
    scores = dot_nt(key, query) * EXP_SCALE + bias
    top = jnp.max(scores, axis=0, keepdims=True)
    unnormed = jnp.exp2(scores - top)
    total = jnp.sum(unnormed, axis=0, keepdims=True)
    return unnormed * (1.0 / total)


def head_score_grad(probs, grad, value):
    prob_grad = dot_nt(value, grad)
    delta = jnp.sum(probs * prob_grad, axis=0, keepdims=True)
    return (probs * (prob_grad - delta)).astype(jnp.bfloat16)


def columns(head):
    return pl.ds(pl.multiple_of(head * HD, HD), HD)


def kernel(
    head_count, lengths, q_hbm, k_hbm, v_hbm, g_hbm, dq_out_ref, dk_out_ref, dv_out_ref,
    q_own, k_own, v_own, g_own, landed, back, partial, own_sum, done, bias, kept,
    load_sem, send_sem, land_sem, partial_send, partial_recv, final_send, final_recv,
):
    me = lax.axis_index("group")
    rows = q_hbm.shape[0]
    spans = lengths.shape[0]
    span_len = 4 * rows // spans
    inputs = ((k_hbm, k_own), (v_hbm, v_own), (q_hbm, q_own), (g_hbm, g_own))
    outputs = (dq_out_ref, dk_out_ref, dv_out_ref)

    def load(which):
        return pltpu.make_async_copy(inputs[which][0], inputs[which][1], load_sem.at[which])

    def forward(which, slot, sender_slot, target, head):
        return pltpu.make_async_remote_copy(
            src_ref=inputs[which][0].at[:, columns(head)],
            dst_ref=landed.at[slot, head],
            send_sem=send_sem.at[sender_slot, head],
            recv_sem=land_sem.at[slot, head],
            device_id={"group": target},
            device_id_type=MESH,
        )

    def give_back(pair, lane, which, target, head):
        return pltpu.make_async_remote_copy(
            src_ref=back.at[pair, which, head],
            dst_ref=partial.at[lane, which, head],
            send_sem=partial_send.at[pair, which, head],
            recv_sem=partial_recv.at[lane, which, head],
            device_id={"group": target},
            device_id_type=MESH,
        )

    def finish(which, head):
        return pltpu.make_async_remote_copy(
            src_ref=done.at[which, head],
            dst_ref=outputs[which].at[:, columns(head)],
            send_sem=final_send.at[which, head],
            recv_sem=final_recv.at[which, head],
            device_id={"group": 3},
            device_id_type=MESH,
        )

    def greet(peers):
        barrier = pltpu.get_barrier_semaphore()
        for peer in peers:
            pl.semaphore_signal(barrier, inc=1, device_id={"group": peer}, device_id_type=MESH)
        pl.semaphore_wait(barrier, len(peers))

    def each_head(step):
        lax.fori_loop(0, head_count, lambda head, carry: (step(head), carry)[1], 0)

    def make_masks(first_query, query_count, key_count):
        shape = (key_count, query_count)
        key_at = lax.broadcasted_iota(jnp.int32, shape, 0)
        query_at = lax.broadcasted_iota(jnp.int32, shape, 1) + first_query
        row_at = lax.broadcasted_iota(jnp.int32, (query_count, HD), 0) + first_query
        key_span = jnp.zeros(shape, jnp.int32)
        query_span = jnp.zeros(shape, jnp.int32)
        key_end = jnp.zeros(shape, jnp.int32)
        row_end = jnp.zeros((query_count, HD), jnp.int32)
        for span in range(spans):
            start = span * span_len
            end = start + lengths[span]
            key_span = jnp.where(key_at >= start, span, key_span)
            query_span = jnp.where(query_at >= start, span, query_span)
            key_end = jnp.where(key_at >= start, end, key_end)
            row_end = jnp.where(row_at >= start, end, row_end)
        visible = (key_span <= query_span) & (key_at < key_end)
        bias[:key_count, :query_count] = jnp.where(visible, 0.0, masked_score)
        kept[:query_count, :] = jnp.where(row_at < row_end, 1.0, 0.0).astype(jnp.bfloat16)

    @pl.when(me != 3)
    def _():
        for which in range(4):
            load(which).start()

    def wait_loads():
        for which in range(4):
            load(which).wait()

    def low(value):
        return value.astype(jnp.bfloat16)

    @pl.when(me == 0)
    def _():
        greet((1, 2))

        def send(head):
            for which in range(2):
                forward(which, which, 2 + which, 1, head).start()
                forward(which, which, which, 2, head).start()

        each_head(send)
        make_masks(0, rows, rows)
        wait_loads()

        def own(head):
            at = columns(head)
            query, key = q_own[:, at], k_own[:, at]
            grad = g_own[:, at] * kept[:rows, :]
            probs = head_probs(query, key, bias[:rows, :rows])
            own_sum[1, head] = dot_nn(low(probs), grad)
            score_grad = head_score_grad(probs, grad, v_own[:, at])
            own_sum[0, head] = dot_nn(score_grad, query) * SCALE
            dq_out_ref[:, at] = low(dot_tn(score_grad, key) * SCALE)

        each_head(own)

        def gather(head):
            at = columns(head)
            for which in (1, 0):
                give_back(0, 0, which, 0, head).wait_recv()
                give_back(0, 1, which, 0, head).wait_recv()
                outputs[1 + which][:, at] = low(
                    own_sum[which, head]
                    + partial[0, which, head].astype(jnp.float32)
                    + partial[1, which, head].astype(jnp.float32)
                )

        each_head(gather)

        def settle(head):
            for which in range(2):
                forward(which, which, which, 2, head).wait_send()
                forward(which, which, 2 + which, 1, head).wait_send()

        each_head(settle)

    @pl.when(me == 1)
    def _():
        greet((0, 2))

        def send(head):
            for which in range(2):
                forward(which, 2 + which, which, 2, head).start()

        each_head(send)
        make_masks(rows, rows, 2 * rows)
        wait_loads()

        def work(head):
            at = columns(head)
            query = q_own[:, at]
            grad = g_own[:, at] * kept[:rows, :]
            forward(0, 0, 2, 1, head).wait_recv()
            key = jnp.concatenate([landed[0, head], k_own[:, at]], axis=0)
            probs = head_probs(query, key, bias[: 2 * rows, :rows])
            dv = dot_nn(low(probs), grad)
            back[0, 1, head] = low(dv[:rows])
            give_back(0, 0, 1, 0, head).start()
            own_sum[1, head] = dv[rows:]
            forward(1, 1, 3, 1, head).wait_recv()
            value = jnp.concatenate([landed[1, head], v_own[:, at]], axis=0)
            score_grad = head_score_grad(probs, grad, value)
            dk = dot_nn(score_grad, query) * SCALE
            back[0, 0, head] = low(dk[:rows])
            give_back(0, 0, 0, 0, head).start()
            own_sum[0, head] = dk[rows:]
            dq_out_ref[:, at] = low(dot_tn(score_grad, key) * SCALE)

        each_head(work)

        def gather(head):
            at = columns(head)
            for which in (1, 0):
                give_back(1, 0, which, 1, head).wait_recv()
                outputs[1 + which][:, at] = low(
                    own_sum[which, head] + partial[0, which, head].astype(jnp.float32)
                )

        each_head(gather)

        def settle(head):
            for which in range(2):
                forward(which, 2 + which, which, 2, head).wait_send()
            for which in range(2):
                give_back(0, 0, which, 0, head).wait_send()

        each_head(settle)

    @pl.when(me == 2)
    def _():
        greet((0, 1, 3))
        make_masks(2 * rows, 2 * rows, 4 * rows)
        wait_loads()

        def work(head):
            at = columns(head)

            def arrive(which, slot):
                forward(which, slot, which, 2, head).wait_recv()

            def give(which, grad_sum):
                for target in range(2):
                    mine = slice(target * rows, (target + 1) * rows)
                    back[target, which, head] = low(grad_sum[mine])
                    give_back(target, 1 - target, which, target, head).start()
                done[1 + which, head] = low(grad_sum[3 * rows :])
                finish(1 + which, head).start()
                outputs[1 + which][:, at] = low(grad_sum[2 * rows : 3 * rows])

            arrive(2, 6)
            arrive(3, 7)
            arrive(0, 4)
            arrive(0, 0)
            arrive(0, 2)
            query = jnp.concatenate([q_own[:, at], landed[6, head]], axis=0)
            grad = jnp.concatenate([g_own[:, at], landed[7, head]], axis=0) * kept[...]
            key = jnp.concatenate(
                [landed[0, head], landed[2, head], k_own[:, at], landed[4, head]], axis=0
            )
            probs = head_probs(query, key, bias[...])
            give(1, dot_nn(low(probs), grad))
            arrive(1, 5)
            arrive(1, 1)
            arrive(1, 3)
            value = jnp.concatenate(
                [landed[1, head], landed[3, head], v_own[:, at], landed[5, head]], axis=0
            )
            score_grad = head_score_grad(probs, grad, value)
            give(0, dot_nn(score_grad, query) * SCALE)
            dq = dot_tn(score_grad, key) * SCALE
            dq_out_ref[:, at] = low(dq[:rows])
            done[0, head] = low(dq[rows:])
            finish(0, head).start()

        each_head(work)

        def settle(head):
            for target in range(2):
                for which in range(2):
                    give_back(target, 1 - target, which, target, head).wait_send()
            for which in range(3):
                finish(which, head).wait_send()

        each_head(settle)

    @pl.when(me == 3)
    def _():
        greet((2,))

        def send(head):
            for which in (0, 2, 3, 1):
                forward(which, 4 + which, which, 2, head).start()

        each_head(send)

        def settle(head):
            for which in range(4):
                forward(which, 4 + which, which, 2, head).wait_send()
            for which in range(3):
                finish(which, head).wait_recv()

        each_head(settle)


def four_slices(queries, keys, values, grad_out, lengths):
    rows, features = queries.shape
    heads = features // HD
    low_type = jnp.bfloat16
    out = jax.ShapeDtypeStruct((rows, features), low_type)
    anywhere = pl.BlockSpec(memory_space=pl.ANY)
    dma = pltpu.SemaphoreType.DMA
    return pl.pallas_call(
        functools.partial(kernel, heads),
        out_shape=(pltpu.VMEM((rows, features), low_type),) * 3,
        in_specs=[pl.BlockSpec(memory_space=pltpu.SMEM)] + [anywhere] * 4,
        out_specs=(pl.BlockSpec(memory_space=pltpu.VMEM),) * 3,
        scratch_shapes=[
            pltpu.VMEM((rows, features), low_type),
            pltpu.VMEM((rows, features), low_type),
            pltpu.VMEM((rows, features), low_type),
            pltpu.VMEM((rows, features), low_type),
            pltpu.VMEM((8, heads, rows, HD), low_type),
            pltpu.VMEM((2, 2, heads, rows, HD), low_type),
            pltpu.VMEM((2, 2, heads, rows, HD), low_type),
            pltpu.VMEM((2, heads, rows, HD), jnp.float32),
            pltpu.VMEM((3, heads, rows, HD), low_type),
            pltpu.VMEM((4 * rows, 2 * rows), jnp.float32),
            pltpu.VMEM((2 * rows, HD), low_type),
            dma((4,)),
            dma((4, heads)),
            dma((8, heads)),
            dma((2, 2, heads)),
            dma((2, 2, heads)),
            dma((3, heads)),
            dma((3, heads)),
        ],
        compiler_params=pltpu.CompilerParams(
            collective_id=0, has_side_effects=True, vmem_limit_bytes=60 * 1024 * 1024
        ),
    )(lengths, queries, keys, values, grad_out)


def solution(mesh):
    return jax.shard_map(
        four_slices if mesh.shape["group"] == 4 else body,
        mesh=mesh,
        in_specs=(
            P(("batch", "group"), "head"),
            P(("batch", "group"), "head"),
            P(("batch", "group"), "head"),
            P(("batch", "group"), "head"),
            P("batch"),
        ),
        out_specs=(
            P(("batch", "group"), "head"),
            P(("batch", "group"), "head"),
            P(("batch", "group"), "head"),
        ),
        check_vma=False,
    )
```
